32 devices in a mesh: dp: 2 (over core), chan: 4 (over z), seq: 4 (over y, x).
Axes of the slice: x: 2, y: 2, z: 4, core: 2. Of those that a mesh axis runs over, the one named last changes fastest.
Arguments:
- query_proj: bfloat16 [2, 2048, 2048], P('dp', 'chan', 'seq'), may hold values from -6 to 6
- key_proj: bfloat16 [2, 2048, 2048], P('dp', 'chan', 'seq'), may hold values from -6 to 6
- value_proj: bfloat16 [2, 2048, 2048], P('dp', 'chan', 'seq'), may hold values from -6 to 6
- grad_out: bfloat16 [2, 2048, 2048], P('dp', 'chan', 'seq'), may hold values from -6 to 6
- out_weight: bfloat16 [2048, 2048], P('chan'), may hold values from -0.125 to 0.125
- long_filter: float32 [2048, 2048], P(('chan', 'seq')), may hold values from -2 to 2, as said below
Outputs:
- grad_query: bfloat16 [2, 2048, 2048], P('dp', 'chan', 'seq')
- grad_key: bfloat16 [2, 2048, 2048], P('dp', 'chan', 'seq')
- grad_value: bfloat16 [2, 2048, 2048], P('dp', 'chan', 'seq')
- grad_weight: float32 [2048, 2048], P('chan')
The draws below stay inside these ranges and needn't reach their ends.
Inputs may be any that keep to these rules, and one draw needn't show every extreme that they name: `long_filter`: taps of each channel's causal filter.
All inputs are finite; a program needn't handle non-finite values.
Results may differ from the reference program's by a relative error of at most 0.0029.
Values may be sent and summed in bfloat16 or wider, within the bound.
A program may use at most 64 MiB of HBM per device.

```python
import math
import jax
import jax.numpy as jnp
from jax import lax

CH = 2048
SEQLEN = 2048
BATCH = 2


def draw_long_filter(key, part):
    key_kind, key_slow, key_fast, key_noise = jax.random.split(key, 4)
    share = 0.5
    noise = jnp.clip(jax.random.normal(key_noise, (CH, SEQLEN), jnp.float32), -6.0, 6.0)
    slow_mask = jax.random.bernoulli(key_kind, share, (CH, 1))
    slow_rate = jnp.exp(jax.random.uniform(key_slow, (CH, 1), jnp.float32, math.log(0.3), math.log(2.0))) / SEQLEN
    fast_rate = jnp.exp(jax.random.uniform(key_fast, (CH, 1), jnp.float32, math.log(1.0 / 50.0), math.log(1.0 / 30.0)))
    rate = jnp.where(slow_mask, slow_rate, fast_rate)
    positions = lax.broadcasted_iota(jnp.float32, (CH, SEQLEN), 1)
    amplitude = jnp.sqrt(2.0 * rate / (1.0 - jnp.exp(-2.0 * rate * SEQLEN)))
    return (noise * amplitude * jnp.exp(-rate * positions)).astype(jnp.float32)


def shard_levels(own_key, shape, cuts, least, high):
    factor_of = 1.0
    for position, blocks in cuts:
        draws = jax.random.uniform(jax.random.fold_in(jax.random.fold_in(own_key, 6), position), (blocks,), jnp.float32, least / len(cuts), high / len(cuts))
        factor_of = factor_of * jnp.repeat(jnp.exp(draws), shape[position] // blocks).reshape((-1,) + (1,) * (len(shape) - 1 - position))
    return factor_of


def gaussian(own_key, shape, width, reach, shards=(), dtype=jnp.bfloat16):
    drawn = width * jax.random.normal(own_key, shape, jnp.float32)
    if shards:
        drawn = drawn * shard_levels(own_key, shape, shards, -0.22, 0.18)
    return jnp.clip(drawn, -reach, reach).astype(dtype)


def setup_inputs(seed: int = 0) -> dict:
    arg_keys = jax.random.split(jax.random.key(seed), 7)
    return {
        "query_proj": gaussian(arg_keys[0], (BATCH, CH, SEQLEN), 1.0, 6.0, ((0, 2), (1, 4), (2, 4))),
        "key_proj": gaussian(arg_keys[1], (BATCH, CH, SEQLEN), 1.0, 6.0, ((0, 2), (1, 4), (2, 4))),
        "value_proj": gaussian(arg_keys[2], (BATCH, CH, SEQLEN), 1.0, 6.0, ((0, 2), (1, 4), (2, 4))),
        "grad_out": gaussian(arg_keys[3], (BATCH, CH, SEQLEN), 1.0, 6.0, ((0, 2), (1, 4), (2, 4))),
        "out_weight": gaussian(arg_keys[4], (CH, CH), CH ** -0.5, 0.125, ((0, 4),)),
        "long_filter": draw_long_filter(jax.random.fold_in(arg_keys[6], 71), 0),
    }


def spectral(filt_rows, signal, conjugate):
    length = signal.shape[-1]
    total_len = 2 * length
    filt_spec = jnp.fft.rfft(filt_rows, n=total_len)
    signal_spec = jnp.fft.rfft(signal, n=total_len)
    if conjugate:
        filt_spec = jnp.conj(filt_spec)
    return jnp.fft.irfft(signal_spec * filt_spec, n=total_len)[..., :length]

def channel_map(long_filter, signal, conjugate):
    group_size = min(CH, 128)
    filt_blocks = long_filter.reshape(CH // group_size, group_size, SEQLEN)
    signal_blocks = signal.reshape(CH // group_size, group_size, SEQLEN)
    result = lax.map(lambda pair: spectral(pair[0], pair[1], conjugate), (filt_blocks, signal_blocks))
    return result.reshape(CH, SEQLEN).astype(jnp.float32)

def reference(query_proj, key_proj, value_proj, grad_out, out_weight, long_filter):
    weight_total = jnp.zeros((CH, CH), jnp.float32)
    query_list = []
    key_list = []
    value_list = []
    for seq_index in range(BATCH):
        query_vals = query_proj[seq_index].astype(jnp.float32)
        key_vals = key_proj[seq_index].astype(jnp.float32)
        value_vals = value_proj[seq_index].astype(jnp.float32)
        mixed_in = key_vals * value_vals
        conv_out = channel_map(long_filter, mixed_in, False)
        gated_out = (query_vals * conv_out).astype(jnp.bfloat16)
        grad_mid = jnp.dot(out_weight, grad_out[seq_index], preferred_element_type=jnp.float32)
        weight_total = weight_total + lax.dot_general(gated_out, grad_out[seq_index], (((1,), (1,)), ((), ())), preferred_element_type=jnp.float32)
        grad_gate = query_vals * grad_mid
        query_list.append((grad_mid * conv_out).astype(jnp.bfloat16))
        back_out = channel_map(long_filter, grad_gate, True)
        key_list.append((back_out * value_vals).astype(jnp.bfloat16))
        value_list.append((back_out * key_vals).astype(jnp.bfloat16))
    grad_weight = weight_total * (1.0 / math.sqrt(BATCH * SEQLEN))
    return (jnp.stack(query_list), jnp.stack(key_list), jnp.stack(value_list), grad_weight)
```

```python
import functools
import math

import jax
import jax.numpy as jnp
import numpy as np
from jax import lax
from jax.experimental import pallas as pl
from jax.experimental.pallas import tpu as pltpu
from jax.sharding import PartitionSpec as P

LANES = 128
MESH = pl.DeviceIdType.MESH
VMEM_LIMIT = 56 * 1024 * 1024


def split_table(table):
    high = table.astype(jnp.bfloat16)
    low = (table - high.astype(np.float64)).astype(jnp.bfloat16)
    return [high, low]


def make_tables(slabs):
    total = 2 * slabs * LANES
    lane = np.arange(LANES, dtype=np.float64)
    turn = 2.0 * np.pi / LANES * (np.outer(lane, lane) % LANES)
    cos_lane, sin_lane = np.cos(turn), np.sin(turn)
    ahead = np.block([[cos_lane, -sin_lane], [sin_lane, cos_lane]])
    back = np.block([[cos_lane, sin_lane], [-sin_lane, cos_lane]]) / total
    twist = 2.0 * np.pi / total * np.outer(np.arange(slabs + 1, dtype=np.float64), lane)
    wide = lambda rows: np.broadcast_to(rows[:, None, :], (slabs + 1, 8, LANES)).astype(np.float32)
    return split_table(ahead) + split_table(back) + [wide(np.cos(twist)), wide(np.sin(twist))]


def add(left, right):
    if left is None:
        return right
    if right is None:
        return left
    return left + right


def sub(left, right):
    if right is None:
        return left
    if left is None:
        return -right
    return left - right


def mul(value, factor):
    return None if value is None else value * factor


def half_fft(size, points):
    if size == 2:
        return [(points[0], None), (points[0], None)]
    even, odd = half_fft(size // 2, points[::2]), half_fft(size // 2, points[1::2])
    bins = [None] * (size // 2 + 1)
    for k in range(size // 4 + 1):
        (e_re, e_im), (o_re, o_im) = even[k], odd[k]
        if k == 0:
            t_re, t_im = o_re, None
        elif k == size // 4:
            t_re, t_im = None, -o_re
        else:
            cos, sin = math.cos(2 * math.pi * k / size), math.sin(2 * math.pi * k / size)
            t_re = add(mul(o_re, cos), mul(o_im, sin))
            t_im = sub(mul(o_im, cos), mul(o_re, sin))
        if k != size // 4:
            bins[size // 2 - k] = (sub(e_re, t_re), sub(t_im, e_im))
        bins[k] = (add(e_re, t_re), add(e_im, t_im))
    return bins


def half_inverse(size, bins):
    if size == 2:
        return [bins[0][0] + bins[1][0]]
    even, odd = [], []
    for k in range(size // 4 + 1):
        (u_re, u_im), (v_re, v_im) = bins[k], bins[size // 2 - k]
        if k == 0:
            even.append((u_re + v_re, None))
            odd.append((u_re - v_re, None))
        elif k == size // 4:
            even.append((u_re + u_re, None))
            odd.append((-(u_im + u_im), None))
        else:
            cos, sin = math.cos(2 * math.pi * k / size), math.sin(2 * math.pi * k / size)
            d_re, d_im = u_re - v_re, add(u_im, v_im)
            even.append((u_re + v_re, sub(u_im, v_im)))
            odd.append((sub(d_re * cos, mul(d_im, sin)), add(d_re * sin, mul(d_im, cos))))
    points = [None] * (size // 2)
    points[::2], points[1::2] = half_inverse(size // 2, even), half_inverse(size // 2, odd)
    return points


def pass_rows(rows):
    return max(d for d in range(8, 577, 8) if rows % d == 0)


def three_dot(wide, high, low):
    big = wide.astype(jnp.bfloat16)
    small = (wide - big.astype(jnp.float32)).astype(jnp.bfloat16)
    dot = functools.partial(jnp.dot, preferred_element_type=jnp.float32)
    return dot(big, high) + (dot(small, high) + dot(big, low))


def slab_pass(load, spec, cos_ref, sin_ref, slabs, width):
    @pl.loop(0, width // 8)
    def _(step):
        row = pl.multiple_of(step * 8, 8)
        bins = half_fft(2 * slabs, [load(a, row) for a in range(slabs)])
        for k, (re, im) in enumerate(bins):
            cos, sin = cos_ref[k], sin_ref[k]
            rows = pl.ds(pl.multiple_of(k * width + row, 8), 8)
            spec[rows, :LANES] = add(re * cos, mul(im, sin))
            spec[rows, LANES:] = sub(mul(im, cos), re * sin)


def lane_pass(spec, out, ahead):
    rows = pass_rows(spec.shape[0])

    @pl.loop(0, spec.shape[0] // rows)
    def _(step):
        part = pl.ds(pl.multiple_of(step * rows, 8), rows)
        out[part, :] = three_dot(spec[part, :], ahead[0][...], ahead[1][...])


def filter_pass(spec, filt, ahead, back, conjugate):
    rows = pass_rows(spec.shape[0])

    @pl.loop(0, spec.shape[0] // rows)
    def _(step):
        part = pl.ds(pl.multiple_of(step * rows, 8), rows)
        signal = three_dot(spec[part, :], ahead[0][...], ahead[1][...])
        s_re, s_im = signal[:, :LANES], signal[:, LANES:]
        f_re, f_im = filt[part, :LANES], filt[part, LANES:]
        if conjugate:
            p_re, p_im = s_re * f_re + s_im * f_im, s_im * f_re - s_re * f_im
        else:
            p_re, p_im = s_re * f_re - s_im * f_im, s_im * f_re + s_re * f_im
        product = jnp.concatenate([p_re, p_im], axis=1)
        spec[part, :] = three_dot(product, back[0][...], back[1][...])


def slab_inverse(spec, full, cos_ref, sin_ref, slabs, width):
    @pl.loop(0, width // 8)
    def _(step):
        row = pl.multiple_of(step * 8, 8)
        bins = []
        for k in range(slabs + 1):
            rows = pl.ds(pl.multiple_of(k * width + row, 8), 8)
            re, im = spec[rows, :LANES], spec[rows, LANES:]
            cos, sin = cos_ref[k], sin_ref[k]
            bins.append((re * cos - im * sin, re * sin + im * cos))
        for a, point in enumerate(half_inverse(2 * slabs, bins)):
            full[a, pl.ds(row, 8), :] = point


def push(src, dst, sems, slot, device):
    copy = pltpu.make_async_remote_copy(
        src_ref=src, dst_ref=dst, send_sem=sems.at[0, slot], recv_sem=sems.at[1, slot],
        device_id=device, device_id_type=MESH,
    )
    copy.start()
    return copy


def greet(devices):
    barrier = pltpu.get_barrier_semaphore()
    for device in devices:
        pl.semaphore_signal(barrier, inc=1, device_id=device, device_id_type=MESH)
    pl.semaphore_wait(barrier, len(devices))


def forward_kernel(n, key_ref, value_ref, filt_ref, ah, al, bh, bl, cos_ref, sin_ref,
                   conv, fspec, mixed, full, spec, out_sems, back_sems):
    me = lax.axis_index("seq")
    local, channels = mixed.shape[0], mixed.shape[1]
    width, slabs = channels // n, local * n
    peers = [lax.rem(me + r, n) for r in range(1, n)]
    greet([{"seq": p} for p in peers])

    def slab_ids(p):
        return pl.ds(p * local, local)

    def channel_ids(p):
        return pl.ds(pl.multiple_of(p * width, width), width)

    waits = []
    for slot, p in enumerate(peers + [me]):
        rows = channel_ids(p)
        product = key_ref[rows, :].astype(jnp.float32) * value_ref[rows, :].astype(jnp.float32)
        for l in range(local):
            piece = product[:, l * LANES:(l + 1) * LANES]
            if slot < n - 1:
                mixed[l, rows, :] = piece
            else:
                full[me * local + l] = piece
        if slot < n - 1:
            waits.append(push(mixed.at[:, rows, :], full.at[slab_ids(me)], out_sems, slot, {"seq": p}))
    slab_pass(lambda a, row: filt_ref[pl.ds(row, 8), a * LANES:(a + 1) * LANES], spec, cos_ref, sin_ref, slabs, width)
    lane_pass(spec, fspec, (ah, al))
    for copy in waits:
        copy.wait()
    slab_pass(lambda a, row: full[a, pl.ds(row, 8), :], spec, cos_ref, sin_ref, slabs, width)
    filter_pass(spec, fspec, (ah, al), (bh, bl), False)
    slab_inverse(spec, full, cos_ref, sin_ref, slabs, width)
    waits = []
    for slot, p in enumerate(peers):
        waits.append(push(full.at[slab_ids(p)], conv.at[:, channel_ids(me), :], back_sems, slot, {"seq": p}))
    for l in range(local):
        conv[l, channel_ids(me), :] = full[me * local + l]
    for copy in waits:
        copy.wait()


def backward_kernel(n, scale, query_ref, key_ref, value_ref, weight_ref, grad_ref, conv, fspec,
                    ah, al, bh, bl, cos_ref, sin_ref,
                    grad_query, grad_key, grad_value, grad_weight,
                    gate, full, back, turned, spec, gated, pair_send, pair_recv, own_part, ring_send, ring_recv,
                    out_sems, back_sems, pair_sems, ring_sems, share_sems, final_sems):
    me, core = lax.axis_index("seq"), lax.axis_index("dp")
    local, channels = gate.shape[0], gate.shape[1]
    width, slabs = channels // n, local * n
    half, cols = channels // 2, grad_weight.shape[1] // n
    peers = [lax.rem(me + r, n) for r in range(1, n)]
    other = {"dp": 1 - core}
    greet([{"seq": p} for p in peers] + [other])

    def slab_ids(p):
        return pl.ds(p * local, local)

    def channel_ids(p):
        return pl.ds(pl.multiple_of(p * width, width), width)

    waits = []
    for slot, p in enumerate(peers + [me]):
        rows = channel_ids(p)
        mid = jnp.dot(weight_ref[rows, :], grad_ref[...], preferred_element_type=jnp.float32)
        query = query_ref[rows, :].astype(jnp.float32)
        for l in range(local):
            lanes = slice(l * LANES, (l + 1) * LANES)
            mid_l, query_l, conv_l = mid[:, lanes], query[:, lanes], conv[l, rows, :]
            if slot < n - 1:
                gate[l, rows, :] = query_l * mid_l
            else:
                full[me * local + l] = query_l * mid_l
            grad_query[rows, lanes] = (mid_l * conv_l).astype(jnp.bfloat16)
            gated[rows, lanes] = (query_l * conv_l).astype(jnp.bfloat16)
        if slot < n - 1:
            waits.append(push(gate.at[:, rows, :], full.at[slab_ids(me)], out_sems, slot, {"seq": p}))

    def weight_half(which, dest):
        rows = pl.ds(pl.multiple_of(which * half, half), half)

        @pl.loop(0, n)
        def _(step):
            dest[step] = lax.dot_general(
                gated[rows, :], grad_ref[pl.ds(pl.multiple_of(step * cols, cols), cols), :],
                (((1,), (1,)), ((), ())), preferred_element_type=jnp.float32,
            )

    weight_half(1 - core, pair_send)
    pair = push(pair_send, pair_recv, pair_sems, 0, other)
    weight_half(core, own_part)
    pair.wait()
    ring = []
    for slot, p in enumerate(peers):
        ring_send[slot] = (own_part[p] + pair_recv[p]).astype(jnp.bfloat16)
        ring.append(push(ring_send.at[slot], ring_recv.at[slot], ring_sems, slot, {"seq": p}))

    for copy in waits:
        copy.wait()
    slab_pass(lambda a, row: full[a, pl.ds(row, 8), :], spec, cos_ref, sin_ref, slabs, width)
    filter_pass(spec, fspec, (ah, al), (bh, bl), True)
    slab_inverse(spec, back, cos_ref, sin_ref, slabs, width)
    waits = []
    for slot, p in enumerate(peers):
        waits.append(push(back.at[slab_ids(p)], turned.at[:, channel_ids(me), :], back_sems, slot, {"seq": p}))
    for l in range(local):
        turned[l, channel_ids(me), :] = back[me * local + l]

    total = own_part[me] + pair_recv[me]
    for slot, copy in enumerate(ring):
        copy.wait()
        total = total + ring_recv[slot].astype(jnp.float32)
    mine = pl.ds(pl.multiple_of(core * half, half), half)

    def chunk(p):
        return grad_weight.at[mine, pl.ds(pl.multiple_of(p * cols, cols), cols)]

    chunk(me)[...] = (total * scale).astype(jnp.bfloat16)
    share = [push(chunk(me), chunk(me), share_sems, slot, {"seq": p}) for slot, p in enumerate(peers)]
    final = [push(chunk(me), chunk(me), final_sems, n - 1, other)]

    for copy in waits:
        copy.wait()
    for l in range(local):
        lanes = slice(l * LANES, (l + 1) * LANES)
        mixed = turned[l]
        grad_key[:, lanes] = (mixed * value_ref[:, lanes].astype(jnp.float32)).astype(jnp.bfloat16)
        grad_value[:, lanes] = (mixed * key_ref[:, lanes].astype(jnp.float32)).astype(jnp.bfloat16)
    for slot, copy in enumerate(share):
        copy.wait()
        source = lax.rem(me + n - slot - 1, n)
        final.append(push(chunk(source), chunk(source), final_sems, slot, other))
    for copy in final:
        copy.wait()


def sems(count):
    return pltpu.SemaphoreType.DMA((2, count))


def shards(query_proj, key_proj, value_proj, grad_out, out_weight, long_filter):
    n = lax.axis_size("seq")
    channels, positions = query_proj.shape[1:]
    local = positions // LANES
    slabs, width = local * n, channels // n
    spec_rows = (slabs + 1) * width
    features = out_weight.shape[1]
    tables = [jnp.asarray(t) for t in make_tables(slabs)]
    vmem = pl.BlockSpec(memory_space=pltpu.VMEM)
    f32, bf16 = jnp.float32, jnp.bfloat16

    pieces = lax.all_gather(grad_out[0], "chan", axis=0, tiled=True)
    fft_flops = 12 * spec_rows * 256 * 256
    conv, fspec = pl.pallas_call(
        functools.partial(forward_kernel, n),
        out_shape=(
            jax.ShapeDtypeStruct((local, channels, LANES), f32),
            jax.ShapeDtypeStruct((spec_rows, 2 * LANES), f32),
        ),
        in_specs=[vmem] * 9,
        out_specs=(vmem, vmem),
        scratch_shapes=[
            pltpu.VMEM((local, channels, LANES), f32),
            pltpu.VMEM((slabs, width, LANES), f32),
            pltpu.VMEM((spec_rows, 2 * LANES), f32),
            sems(n - 1), sems(n - 1),
        ],
        compiler_params=pltpu.CompilerParams(
            collective_id=0, has_side_effects=True, vmem_limit_bytes=VMEM_LIMIT
        ),
        cost_estimate=pl.CostEstimate(flops=20 * fft_flops, bytes_accessed=64 * channels * positions, transcendentals=0),
        name="forward",
    )(key_proj[0], value_proj[0], long_filter, *tables)

    scale = 1.0 / math.sqrt(lax.axis_size("dp") * long_filter.shape[1])
    half, cols = channels // 2, features // n
    block = jax.ShapeDtypeStruct((channels, positions), bf16)
    grad_query, grad_key, grad_value, grad_weight = pl.pallas_call(
        functools.partial(backward_kernel, n, scale),
        out_shape=(block, block, block, jax.ShapeDtypeStruct((channels, features), bf16)),
        in_specs=[vmem] * 13,
        out_specs=(vmem,) * 4,
        scratch_shapes=[
            pltpu.VMEM((local, channels, LANES), f32),
            pltpu.VMEM((slabs, width, LANES), f32),
            pltpu.VMEM((slabs, width, LANES), f32),
            pltpu.VMEM((local, channels, LANES), f32),
            pltpu.VMEM((spec_rows, 2 * LANES), f32),
            pltpu.VMEM((channels, positions), bf16),
            pltpu.VMEM((n, half, cols), f32),
            pltpu.VMEM((n, half, cols), f32),
            pltpu.VMEM((n, half, cols), f32),
            pltpu.VMEM((n - 1, half, cols), bf16),
            pltpu.VMEM((n - 1, half, cols), bf16),
            sems(n - 1), sems(n - 1), sems(1), sems(n - 1), sems(n - 1), sems(n),
        ],
        compiler_params=pltpu.CompilerParams(
            collective_id=1, has_side_effects=True, vmem_limit_bytes=VMEM_LIMIT
        ),
        cost_estimate=pl.CostEstimate(flops=20 * fft_flops, bytes_accessed=64 * channels * positions, transcendentals=0),
        name="backward",
    )(query_proj[0], key_proj[0], value_proj[0], out_weight, pieces, conv, fspec, *tables)
    return (grad_query[None], grad_key[None], grad_value[None], grad_weight.astype(f32))


def solution(mesh):
    placed = (
        P("dp", "chan", "seq"),
        P("dp", "chan", "seq"),
        P("dp", "chan", "seq"),
        P("dp", "chan", "seq"),
        P("chan", None),
        P(("chan", "seq"), None),
    )
    return jax.shard_map(
        shards,
        mesh=mesh,
        in_specs=placed,
        out_specs=(
            P("dp", "chan", "seq"),
            P("dp", "chan", "seq"),
            P("dp", "chan", "seq"),
            P("chan", None),
        ),
        check_vma=False,
    )
```

```python
import functools
import math

import jax
import jax.numpy as jnp
import numpy as np
from jax import lax
from jax.experimental import pallas as pl
from jax.experimental.pallas import tpu as pltpu
from jax.sharding import PartitionSpec as P

LANES = 128
MESH = pl.DeviceIdType.MESH
VMEM_LIMIT = 56 * 1024 * 1024


def split_table(table):
    high = table.astype(jnp.bfloat16)
    low = (table - high.astype(np.float64)).astype(jnp.bfloat16)
    return [high, low]


def make_tables(slabs):
    total = 2 * slabs * LANES
    lane = np.arange(LANES, dtype=np.float64)
    turn = 2.0 * np.pi / LANES * (np.outer(lane, lane) % LANES)
    cos_lane, sin_lane = np.cos(turn), np.sin(turn)
    ahead = np.block([[cos_lane, -sin_lane], [sin_lane, cos_lane]])
    back = np.block([[cos_lane, sin_lane], [-sin_lane, cos_lane]]) / total
    twist = 2.0 * np.pi / total * np.outer(np.arange(slabs + 1, dtype=np.float64), lane)
    wide = lambda rows: np.broadcast_to(rows[:, None, :], (slabs + 1, 8, LANES)).astype(np.float32)
    return split_table(ahead) + split_table(back) + [wide(np.cos(twist)), wide(np.sin(twist))]


def add(left, right):
    if left is None:
        return right
    if right is None:
        return left
    return left + right


def sub(left, right):
    if right is None:
        return left
    if left is None:
        return -right
    return left - right


def mul(value, factor):
    return None if value is None else value * factor


def half_fft(size, points):
    if size == 2:
        return [(points[0], None), (points[0], None)]
    even, odd = half_fft(size // 2, points[::2]), half_fft(size // 2, points[1::2])
    bins = [None] * (size // 2 + 1)
    for k in range(size // 4 + 1):
        (e_re, e_im), (o_re, o_im) = even[k], odd[k]
        if k == 0:
            t_re, t_im = o_re, None
        elif k == size // 4:
            t_re, t_im = None, -o_re
        else:
            cos, sin = math.cos(2 * math.pi * k / size), math.sin(2 * math.pi * k / size)
            t_re = add(mul(o_re, cos), mul(o_im, sin))
            t_im = sub(mul(o_im, cos), mul(o_re, sin))
        if k != size // 4:
            bins[size // 2 - k] = (sub(e_re, t_re), sub(t_im, e_im))
        bins[k] = (add(e_re, t_re), add(e_im, t_im))
    return bins


def half_inverse(size, bins):
    if size == 2:
        return [bins[0][0] + bins[1][0]]
    even, odd = [], []
    for k in range(size // 4 + 1):
        (u_re, u_im), (v_re, v_im) = bins[k], bins[size // 2 - k]
        if k == 0:
            even.append((u_re + v_re, None))
            odd.append((u_re - v_re, None))
        elif k == size // 4:
            even.append((u_re + u_re, None))
            odd.append((-(u_im + u_im), None))
        else:
            cos, sin = math.cos(2 * math.pi * k / size), math.sin(2 * math.pi * k / size)
            d_re, d_im = u_re - v_re, add(u_im, v_im)
            even.append((u_re + v_re, sub(u_im, v_im)))
            odd.append((sub(d_re * cos, mul(d_im, sin)), add(d_re * sin, mul(d_im, cos))))
    points = [None] * (size // 2)
    points[::2], points[1::2] = half_inverse(size // 2, even), half_inverse(size // 2, odd)
    return points


def pass_rows(rows):
    return max(d for d in range(8, 577, 8) if rows % d == 0)


def three_dot(wide, high, low):
    big = wide.astype(jnp.bfloat16)
    small = (wide - big.astype(jnp.float32)).astype(jnp.bfloat16)
    dot = functools.partial(jnp.dot, preferred_element_type=jnp.float32)
    return dot(big, high) + (dot(small, high) + dot(big, low))


def slab_pass(load, spec, cos_ref, sin_ref, slabs, width):
    @pl.loop(0, width // 8)
    def _(step):
        row = pl.multiple_of(step * 8, 8)
        bins = half_fft(2 * slabs, [load(a, row) for a in range(slabs)])
        for k, (re, im) in enumerate(bins):
            cos, sin = cos_ref[k], sin_ref[k]
            rows = pl.ds(pl.multiple_of(k * width + row, 8), 8)
            spec[rows, :LANES] = add(re * cos, mul(im, sin))
            spec[rows, LANES:] = sub(mul(im, cos), re * sin)


def lane_pass(spec, out, ahead):
    rows = pass_rows(spec.shape[0])

    @pl.loop(0, spec.shape[0] // rows)
    def _(step):
        part = pl.ds(pl.multiple_of(step * rows, 8), rows)
        out[part, :] = three_dot(spec[part, :], ahead[0][...], ahead[1][...])


def filter_pass(spec, filt, ahead, back, conjugate):
    rows = pass_rows(spec.shape[0])

    @pl.loop(0, spec.shape[0] // rows)
    def _(step):
        part = pl.ds(pl.multiple_of(step * rows, 8), rows)
        signal = three_dot(spec[part, :], ahead[0][...], ahead[1][...])
        s_re, s_im = signal[:, :LANES], signal[:, LANES:]
        f_re, f_im = filt[part, :LANES], filt[part, LANES:]
        if conjugate:
            p_re, p_im = s_re * f_re + s_im * f_im, s_im * f_re - s_re * f_im
        else:
            p_re, p_im = s_re * f_re - s_im * f_im, s_im * f_re + s_re * f_im
        product = jnp.concatenate([p_re, p_im], axis=1)
        spec[part, :] = three_dot(product, back[0][...], back[1][...])


def slab_inverse(spec, full, cos_ref, sin_ref, slabs, width):
    @pl.loop(0, width // 8)
    def _(step):
        row = pl.multiple_of(step * 8, 8)
        bins = []
        for k in range(slabs + 1):
            rows = pl.ds(pl.multiple_of(k * width + row, 8), 8)
            re, im = spec[rows, :LANES], spec[rows, LANES:]
            cos, sin = cos_ref[k], sin_ref[k]
            bins.append((re * cos - im * sin, re * sin + im * cos))
        for a, point in enumerate(half_inverse(2 * slabs, bins)):
            full[a, pl.ds(row, 8), :] = point


def push(src, dst, sems, slot, device):
    copy = pltpu.make_async_remote_copy(
        src_ref=src, dst_ref=dst, send_sem=sems.at[0, slot], recv_sem=sems.at[1, slot],
        device_id=device, device_id_type=MESH,
    )
    copy.start()
    return copy


def greet(devices):
    barrier = pltpu.get_barrier_semaphore()
    for device in devices:
        pl.semaphore_signal(barrier, inc=1, device_id=device, device_id_type=MESH)
    pl.semaphore_wait(barrier, len(devices))


def kernel(n, nz, parts, scale, query_ref, key_ref, value_ref, own_ref, weight_ref, filt_ref,
           ah, al, bh, bl, cos_ref, sin_ref,
           grad_query, grad_key, grad_value, grad_weight,
           pieces, mixed, full, conv, fspec, spec, gate, gate_full, turned, gated,
           pair_send, pair_recv, own_part, ring_send, ring_recv,
           mix_sems, conv_sems, gate_sems, back_sems, pair_sems, ring_sems, share_sems, final_sems, line_sems,
           own_sem):
    me, core, level = lax.axis_index("seq"), lax.axis_index("dp"), lax.axis_index("chan")
    local, channels = mixed.shape[0], mixed.shape[1]
    width, slabs = channels // n, local * n
    part_width = width // parts
    half, cols = channels // 2, grad_weight.shape[1] // n
    piece = own_ref.shape[0]
    peers = [lax.rem(me + r, n) for r in range(1, n)]
    levels = [lax.rem(level + r, nz) for r in range(1, nz)]
    other = {"dp": 1 - core}
    greet([{"seq": p} for p in peers] + [other] + [{"chan": z} for z in levels])

    def slab_ids(p):
        return pl.ds(p * local, local)

    def channel_ids(p):
        return pl.ds(pl.multiple_of(p * width, width), width)

    def part_ids(p, h):
        return pl.ds(pl.multiple_of(p * width + h * part_width, part_width), part_width)

    def piece_ids(z):
        return pl.ds(pl.multiple_of(z * piece, piece), piece)

    def line(side, distance, hop):
        sign = 1 if side == 0 else -1
        origin = level - sign * (distance - hop)
        target = level + sign * hop
        ok = (origin >= 0) & (origin < nz) & (target >= 0) & (target < nz)
        source = own_ref if distance == hop else pieces.at[piece_ids(lax.rem(origin + nz, nz))]
        copy = pltpu.make_async_remote_copy(
            src_ref=source, dst_ref=pieces.at[piece_ids(lax.rem(origin + nz, nz))],
            send_sem=line_sems.at[0, side, distance - 1], recv_sem=line_sems.at[1, side, distance - 1],
            device_id={"chan": lax.rem(target + nz, nz)}, device_id_type=MESH,
        )
        return ok, copy

    def line_start(side, distance, hop):
        ok, copy = line(side, distance, hop)
        pl.when(ok)(copy.start)

    def line_sent(side, distance, hop):
        ok, copy = line(side, distance, hop)
        pl.when(ok)(copy.wait_send)

    def line_arrived(side, distance):
        origin = level - (1 if side == 0 else -1) * distance
        rows = piece_ids(lax.rem(origin + nz, nz))
        copy = pltpu.make_async_remote_copy(
            src_ref=own_ref, dst_ref=pieces.at[rows],
            send_sem=line_sems.at[0, side, distance - 1], recv_sem=line_sems.at[1, side, distance - 1],
            device_id={"chan": lax.rem(origin + nz, nz)}, device_id_type=MESH,
        )
        pl.when((origin >= 0) & (origin < nz))(copy.wait_recv)

    direct = min(2, nz - 1)
    for distance in range(direct, 0, -1):
        for side in range(2):
            line_start(side, distance, distance)
    keep = pltpu.make_async_copy(own_ref, pieces.at[piece_ids(level)], own_sem)
    keep.start()

    def leave(block, fulls, leg, h):
        return [
            push(block.at[:, part_ids(p, h), :], fulls.at[h, slab_ids(me)], leg, h * (n - 1) + slot, {"seq": p})
            for slot, p in enumerate(peers)
        ]

    def come_home(fulls, block, leg, h):
        copies = [
            push(fulls.at[h, slab_ids(p)], block.at[:, part_ids(me, h), :], leg, h * (n - 1) + slot, {"seq": p})
            for slot, p in enumerate(peers)
        ]
        for l in range(local):
            block[l, part_ids(me, h), :] = fulls[h, me * local + l]
        return copies

    def own_slabs(block, fulls):
        for h in range(parts):
            for l in range(local):
                fulls[h, me * local + l] = block[l, part_ids(me, h), :]

    def convolve(fulls, h, conjugate):
        slab_pass(lambda a, row: fulls[h, a, pl.ds(row, 8), :], spec, cos_ref, sin_ref, slabs, part_width)
        filter_pass(spec, fspec.at[h], (ah, al), (bh, bl), conjugate)
        slab_inverse(spec, fulls.at[h], cos_ref, sin_ref, slabs, part_width)

    out = []
    for p in peers + [me]:
        rows = channel_ids(p)
        product = key_ref[rows, :].astype(jnp.float32) * value_ref[rows, :].astype(jnp.float32)
        for l in range(local):
            mixed[l, rows, :] = product[:, l * LANES:(l + 1) * LANES]
    for h in range(parts):
        out.append(leave(mixed, full, mix_sems, h))
    own_slabs(mixed, full)
    for h in range(parts):
        slab_pass(
            lambda a, row: filt_ref[pl.ds(pl.multiple_of(h * part_width + row, 8), 8), a * LANES:(a + 1) * LANES],
            spec, cos_ref, sin_ref, slabs, part_width,
        )
        lane_pass(spec, fspec.at[h], (ah, al))
    home = []
    for h in range(parts):
        for copy in out[h]:
            copy.wait()
        convolve(full, h, False)
        home.extend(come_home(full, conv, conv_sems, h))
    for distance in range(3, nz):
        for side in range(2):
            line_arrived(side, distance - 1)
            line_start(side, distance, 1)
    for copy in home:
        copy.wait()
    keep.wait()
    for side in range(2):
        for distance in range(1, nz):
            if not 2 <= distance < nz - 1:
                line_arrived(side, distance)
            line_sent(side, distance, distance if distance <= direct else 1)

    out = [[] for _ in range(parts)]
    for slot, p in enumerate(peers + [me]):
        rows = channel_ids(p)
        mid = jnp.dot(weight_ref[rows, :], pieces[...], preferred_element_type=jnp.float32)
        query = query_ref[rows, :].astype(jnp.float32)
        for l in range(local):
            lanes = slice(l * LANES, (l + 1) * LANES)
            mid_l, query_l, conv_l = mid[:, lanes], query[:, lanes], conv[l, rows, :]
            gate[l, rows, :] = query_l * mid_l
            grad_query[rows, lanes] = (mid_l * conv_l).astype(jnp.bfloat16)
            gated[rows, lanes] = (query_l * conv_l).astype(jnp.bfloat16)
        if slot < n - 1:
            out[0].append(push(gate.at[:, part_ids(p, 0), :], gate_full.at[0, slab_ids(me)], gate_sems, slot, {"seq": p}))
    for h in range(1, parts):
        out[h] = leave(gate, gate_full, gate_sems, h)
    own_slabs(gate, gate_full)

    def weight_half(which, dest):
        rows = pl.ds(pl.multiple_of(which * half, half), half)

        @pl.loop(0, n)
        def _(step):
            dest[step] = lax.dot_general(
                gated[rows, :], pieces[pl.ds(pl.multiple_of(step * cols, cols), cols), :],
                (((1,), (1,)), ((), ())), preferred_element_type=jnp.float32,
            )

    weight_half(1 - core, pair_send)
    pair = push(pair_send, pair_recv, pair_sems, 0, other)
    weight_half(core, own_part)

    home, ring = [], []
    for h in range(parts):
        for copy in out[h]:
            copy.wait()
        convolve(gate_full, h, True)
        home.extend(come_home(gate_full, turned, back_sems, h))
        if h == 0:
            pair.wait()
            for slot, p in enumerate(peers):
                ring_send[slot] = (own_part[p] + pair_recv[p]).astype(jnp.bfloat16)
                ring.append(push(ring_send.at[slot], ring_recv.at[slot], ring_sems, slot, {"seq": p}))

    total = own_part[me] + pair_recv[me]
    for slot, copy in enumerate(ring):
        copy.wait()
        total = total + ring_recv[slot].astype(jnp.float32)
    mine = pl.ds(pl.multiple_of(core * half, half), half)

    def chunk(p):
        return grad_weight.at[mine, pl.ds(pl.multiple_of(p * cols, cols), cols)]

    chunk(me)[...] = (total * scale).astype(jnp.bfloat16)
    share = [push(chunk(me), chunk(me), share_sems, slot, {"seq": p}) for slot, p in enumerate(peers)]
    final = [push(chunk(me), chunk(me), final_sems, n - 1, other)]

    for copy in home:
        copy.wait()
    for l in range(local):
        lanes = slice(l * LANES, (l + 1) * LANES)
        back = turned[l]
        grad_key[:, lanes] = (back * value_ref[:, lanes].astype(jnp.float32)).astype(jnp.bfloat16)
        grad_value[:, lanes] = (back * key_ref[:, lanes].astype(jnp.float32)).astype(jnp.bfloat16)
    for slot, copy in enumerate(share):
        copy.wait()
        source = lax.rem(me + n - slot - 1, n)
        final.append(push(chunk(source), chunk(source), final_sems, slot, other))
    for copy in final:
        copy.wait()


def sems(count):
    return pltpu.SemaphoreType.DMA((2, count))


def shards(query_proj, key_proj, value_proj, grad_out, out_weight, long_filter):
    n = lax.axis_size("seq")
    channels, positions = query_proj.shape[1:]
    local = positions // LANES
    slabs, width = local * n, channels // n
    nz = lax.axis_size("chan")
    parts = 2
    part_width = width // parts
    spec_rows = (slabs + 1) * part_width
    features = out_weight.shape[1]
    tables = [jnp.asarray(t) for t in make_tables(slabs)]
    f32, bf16 = jnp.float32, jnp.bfloat16
    scale = 1.0 / math.sqrt(lax.axis_size("dp") * long_filter.shape[1])
    half, cols = channels // 2, features // n
    vmem = pl.BlockSpec(memory_space=pltpu.VMEM)
    block = jax.ShapeDtypeStruct((channels, positions), bf16)
    rows = pltpu.VMEM((local, channels, LANES), f32)
    whole = pltpu.VMEM((parts, slabs, part_width, LANES), f32)
    grad_query, grad_key, grad_value, grad_weight = pl.pallas_call(
        functools.partial(kernel, n, nz, parts, scale),
        out_shape=(block, block, block, jax.ShapeDtypeStruct((channels, features), bf16)),
        in_specs=[vmem] * 12,
        out_specs=(vmem,) * 4,
        scratch_shapes=[
            pltpu.VMEM((features, positions), bf16),
            rows, whole, rows,
            pltpu.VMEM((parts, spec_rows, 2 * LANES), f32),
            pltpu.VMEM((spec_rows, 2 * LANES), f32),
            rows, whole, rows,
            pltpu.VMEM((channels, positions), bf16),
            pltpu.VMEM((n, half, cols), f32),
            pltpu.VMEM((n, half, cols), f32),
            pltpu.VMEM((n, half, cols), f32),
            pltpu.VMEM((n - 1, half, cols), bf16),
            pltpu.VMEM((n - 1, half, cols), bf16),
            sems(parts * (n - 1)), sems(parts * (n - 1)), sems(parts * (n - 1)), sems(parts * (n - 1)),
            sems(1), sems(n - 1), sems(n - 1), sems(n),
            pltpu.SemaphoreType.DMA((2, 2, nz - 1)),
            pltpu.SemaphoreType.DMA(()),
        ],
        compiler_params=pltpu.CompilerParams(
            collective_id=0, has_side_effects=True, vmem_limit_bytes=VMEM_LIMIT
        ),
        cost_estimate=pl.CostEstimate(
            flops=60 * parts * spec_rows * 256 * 256 + 4 * channels * features * positions,
            bytes_accessed=64 * channels * positions, transcendentals=0,
        ),
        name="hyena",
    )(query_proj[0], key_proj[0], value_proj[0], grad_out[0], out_weight, long_filter, *tables)
    return (grad_query[None], grad_key[None], grad_value[None], grad_weight.astype(f32))


def solution(mesh):
    placed = (
        P("dp", "chan", "seq"),
        P("dp", "chan", "seq"),
        P("dp", "chan", "seq"),
        P("dp", "chan", "seq"),
        P("chan", None),
        P(("chan", "seq"), None),
    )
    return jax.shard_map(
        shards,
        mesh=mesh,
        in_specs=placed,
        out_specs=(
            P("dp", "chan", "seq"),
            P("dp", "chan", "seq"),
            P("dp", "chan", "seq"),
            P("chan", None),
        ),
        check_vma=False,
    )
```

```python
import functools
import math

import jax
import jax.numpy as jnp
import numpy as np
from jax import lax
from jax.experimental import pallas as pl
from jax.experimental.pallas import tpu as pltpu
from jax.sharding import PartitionSpec as P

LANES = 128
MESH = pl.DeviceIdType.MESH
VMEM_LIMIT = 56 * 1024 * 1024


def split_table(table):
    high = table.astype(jnp.bfloat16)
    low = (table - high.astype(np.float64)).astype(jnp.bfloat16)
    return [high, low]


def make_tables(slabs):
    total = 2 * slabs * LANES
    lane = np.arange(LANES, dtype=np.float64)
    turn = 2.0 * np.pi / LANES * (np.outer(lane, lane) % LANES)
    cos_lane, sin_lane = np.cos(turn), np.sin(turn)
    ahead = np.block([[cos_lane, -sin_lane], [sin_lane, cos_lane]])
    back = np.block([[cos_lane, sin_lane], [-sin_lane, cos_lane]]) / total
    twist = 2.0 * np.pi / total * np.outer(np.arange(slabs + 1, dtype=np.float64), lane)
    wide = lambda rows: np.broadcast_to(rows[:, None, :], (slabs + 1, 8, LANES)).astype(np.float32)
    return split_table(ahead) + split_table(back) + [wide(np.cos(twist)), wide(np.sin(twist))]


def add(left, right):
    if left is None:
        return right
    if right is None:
        return left
    return left + right


def sub(left, right):
    if right is None:
        return left
    if left is None:
        return -right
    return left - right


def mul(value, factor):
    return None if value is None else value * factor


def half_fft(size, points):
    if size == 2:
        return [(points[0], None), (points[0], None)]
    even, odd = half_fft(size // 2, points[::2]), half_fft(size // 2, points[1::2])
    bins = [None] * (size // 2 + 1)
    for k in range(size // 4 + 1):
        (e_re, e_im), (o_re, o_im) = even[k], odd[k]
        if k == 0:
            t_re, t_im = o_re, None
        elif k == size // 4:
            t_re, t_im = None, -o_re
        else:
            cos, sin = math.cos(2 * math.pi * k / size), math.sin(2 * math.pi * k / size)
            t_re = add(mul(o_re, cos), mul(o_im, sin))
            t_im = sub(mul(o_im, cos), mul(o_re, sin))
        if k != size // 4:
            bins[size // 2 - k] = (sub(e_re, t_re), sub(t_im, e_im))
        bins[k] = (add(e_re, t_re), add(e_im, t_im))
    return bins


def half_inverse(size, bins):
    if size == 2:
        return [bins[0][0] + bins[1][0]]
    even, odd = [], []
    for k in range(size // 4 + 1):
        (u_re, u_im), (v_re, v_im) = bins[k], bins[size // 2 - k]
        if k == 0:
            even.append((u_re + v_re, None))
            odd.append((u_re - v_re, None))
        elif k == size // 4:
            even.append((u_re + u_re, None))
            odd.append((-(u_im + u_im), None))
        else:
            cos, sin = math.cos(2 * math.pi * k / size), math.sin(2 * math.pi * k / size)
            d_re, d_im = u_re - v_re, add(u_im, v_im)
            even.append((u_re + v_re, sub(u_im, v_im)))
            odd.append((sub(d_re * cos, mul(d_im, sin)), add(d_re * sin, mul(d_im, cos))))
    points = [None] * (size // 2)
    points[::2], points[1::2] = half_inverse(size // 2, even), half_inverse(size // 2, odd)
    return points


def pass_rows(rows):
    return max(d for d in range(8, 577, 8) if rows % d == 0)


def three_dot(wide, high, low):
    big = wide.astype(jnp.bfloat16)
    small = (wide - big.astype(jnp.float32)).astype(jnp.bfloat16)
    dot = functools.partial(jnp.dot, preferred_element_type=jnp.float32)
    return dot(big, high) + (dot(small, high) + dot(big, low))


def slab_pass(load, spec, cos_ref, sin_ref, slabs, width):
    @pl.loop(0, width // 8)
    def _(step):
        row = pl.multiple_of(step * 8, 8)
        bins = half_fft(2 * slabs, [load(a, row) for a in range(slabs)])
        for k, (re, im) in enumerate(bins):
            cos, sin = cos_ref[k], sin_ref[k]
            rows = pl.ds(pl.multiple_of(k * width + row, 8), 8)
            spec[rows, :LANES] = add(re * cos, mul(im, sin))
            spec[rows, LANES:] = sub(mul(im, cos), re * sin)


def lane_pass(spec, out, ahead):
    rows = pass_rows(spec.shape[0])

    @pl.loop(0, spec.shape[0] // rows)
    def _(step):
        part = pl.ds(pl.multiple_of(step * rows, 8), rows)
        out[part, :] = three_dot(spec[part, :], ahead[0][...], ahead[1][...])


def filter_pass(spec, filt, ahead, back, conjugate):
    rows = pass_rows(spec.shape[0])

    @pl.loop(0, spec.shape[0] // rows)
    def _(step):
        part = pl.ds(pl.multiple_of(step * rows, 8), rows)
        signal = three_dot(spec[part, :], ahead[0][...], ahead[1][...])
        s_re, s_im = signal[:, :LANES], signal[:, LANES:]
        f_re, f_im = filt[part, :LANES], filt[part, LANES:]
        if conjugate:
            p_re, p_im = s_re * f_re + s_im * f_im, s_im * f_re - s_re * f_im
        else:
            p_re, p_im = s_re * f_re - s_im * f_im, s_im * f_re + s_re * f_im
        product = jnp.concatenate([p_re, p_im], axis=1)
        spec[part, :] = three_dot(product, back[0][...], back[1][...])


def slab_inverse(spec, full, cos_ref, sin_ref, slabs, width):
    @pl.loop(0, width // 8)
    def _(step):
        row = pl.multiple_of(step * 8, 8)
        bins = []
        for k in range(slabs + 1):
            rows = pl.ds(pl.multiple_of(k * width + row, 8), 8)
            re, im = spec[rows, :LANES], spec[rows, LANES:]
            cos, sin = cos_ref[k], sin_ref[k]
            bins.append((re * cos - im * sin, re * sin + im * cos))
        for a, point in enumerate(half_inverse(2 * slabs, bins)):
            full[a, pl.ds(row, 8), :] = point


def push(src, dst, sems, slot, device):
    copy = pltpu.make_async_remote_copy(
        src_ref=src, dst_ref=dst, send_sem=sems.at[0, slot], recv_sem=sems.at[1, slot],
        device_id=device, device_id_type=MESH,
    )
    copy.start()
    return copy


def greet(devices):
    barrier = pltpu.get_barrier_semaphore()
    for device in devices:
        pl.semaphore_signal(barrier, inc=1, device_id=device, device_id_type=MESH)
    pl.semaphore_wait(barrier, len(devices))


def kernel(n, nz, parts, scale, query_ref, key_ref, value_ref, own_ref, weight_ref, filt_ref,
           ah, al, bh, bl, cos_ref, sin_ref,
           grad_query, grad_key, grad_value, grad_weight,
           pieces, mixed, full, conv, fspec, spec, gate, gate_full, turned, gated,
           pair_send, pair_recv, own_part, ring_send, ring_recv,
           mix_sems, conv_sems, gate_sems, back_sems, pair_sems, ring_sems, share_sems, final_sems, line_sems,
           own_sem):
    me, core, level = lax.axis_index("seq"), lax.axis_index("dp"), lax.axis_index("chan")
    local, channels = mixed.shape[0], mixed.shape[1]
    width, slabs = channels // n, local * n
    part_width = width // parts
    half, cols = channels // 2, grad_weight.shape[1] // n
    piece = own_ref.shape[0]
    peers = [lax.rem(me + r, n) for r in range(1, n)]
    levels = [lax.rem(level + r, nz) for r in range(1, nz)]
    other = {"dp": 1 - core}
    greet([{"seq": p} for p in peers] + [other] + [{"chan": z} for z in levels])

    def slab_ids(p):
        return pl.ds(p * local, local)

    def channel_ids(p):
        return pl.ds(pl.multiple_of(p * width, width), width)

    def part_ids(p, h):
        return pl.ds(pl.multiple_of(p * width + h * part_width, part_width), part_width)

    def piece_ids(z):
        return pl.ds(pl.multiple_of(z * piece, piece), piece)

    def line(side, distance, hop):
        sign = 1 if side == 0 else -1
        origin = level - sign * (distance - hop)
        target = level + sign * hop
        ok = (origin >= 0) & (origin < nz) & (target >= 0) & (target < nz)
        source = own_ref if distance == hop else pieces.at[piece_ids(lax.rem(origin + nz, nz))]
        copy = pltpu.make_async_remote_copy(
            src_ref=source, dst_ref=pieces.at[piece_ids(lax.rem(origin + nz, nz))],
            send_sem=line_sems.at[0, side, distance - 1], recv_sem=line_sems.at[1, side, distance - 1],
            device_id={"chan": lax.rem(target + nz, nz)}, device_id_type=MESH,
        )
        return ok, copy

    def line_start(side, distance, hop):
        ok, copy = line(side, distance, hop)
        pl.when(ok)(copy.start)

    def line_sent(side, distance, hop):
        ok, copy = line(side, distance, hop)
        pl.when(ok)(copy.wait_send)

    def line_arrived(side, distance):
        origin = level - (1 if side == 0 else -1) * distance
        rows = piece_ids(lax.rem(origin + nz, nz))
        copy = pltpu.make_async_remote_copy(
            src_ref=own_ref, dst_ref=pieces.at[rows],
            send_sem=line_sems.at[0, side, distance - 1], recv_sem=line_sems.at[1, side, distance - 1],
            device_id={"chan": lax.rem(origin + nz, nz)}, device_id_type=MESH,
        )
        pl.when((origin >= 0) & (origin < nz))(copy.wait_recv)

    for side in range(2):
        line_start(side, 1, 1)
    keep = pltpu.make_async_copy(own_ref, pieces.at[piece_ids(level)], own_sem)
    keep.start()

    def leave(block, fulls, leg, h):
        return [
            push(block.at[:, part_ids(p, h), :], fulls.at[h, slab_ids(me)], leg, h * (n - 1) + slot, {"seq": p})
            for slot, p in enumerate(peers)
        ]

    def come_home(fulls, block, leg, h):
        copies = [
            push(fulls.at[h, slab_ids(p)], block.at[:, part_ids(me, h), :], leg, h * (n - 1) + slot, {"seq": p})
            for slot, p in enumerate(peers)
        ]
        for l in range(local):
            block[l, part_ids(me, h), :] = fulls[h, me * local + l]
        return copies

    def own_slabs(block, fulls):
        for h in range(parts):
            for l in range(local):
                fulls[h, me * local + l] = block[l, part_ids(me, h), :]

    def convolve(fulls, h, conjugate):
        slab_pass(lambda a, row: fulls[h, a, pl.ds(row, 8), :], spec, cos_ref, sin_ref, slabs, part_width)
        filter_pass(spec, fspec.at[h], (ah, al), (bh, bl), conjugate)
        slab_inverse(spec, fulls.at[h], cos_ref, sin_ref, slabs, part_width)

    out = []
    for p in peers + [me]:
        rows = channel_ids(p)
        product = key_ref[rows, :].astype(jnp.float32) * value_ref[rows, :].astype(jnp.float32)
        for l in range(local):
            mixed[l, rows, :] = product[:, l * LANES:(l + 1) * LANES]
    for h in range(parts):
        out.append(leave(mixed, full, mix_sems, h))
    own_slabs(mixed, full)
    for h in range(parts):
        slab_pass(
            lambda a, row: filt_ref[pl.ds(pl.multiple_of(h * part_width + row, 8), 8), a * LANES:(a + 1) * LANES],
            spec, cos_ref, sin_ref, slabs, part_width,
        )
        lane_pass(spec, fspec.at[h], (ah, al))
    home = []
    for h in range(parts):
        for copy in out[h]:
            copy.wait()
        convolve(full, h, False)
        home.extend(come_home(full, conv, conv_sems, h))
        for distance in range(2 + h, nz if h == parts - 1 else min(3 + h, nz)):
            for side in range(2):
                line_arrived(side, distance - 1)
                line_start(side, distance, 1)
    for copy in home:
        copy.wait()
    keep.wait()
    for side in range(2):
        line_arrived(side, nz - 1)
        for distance in range(1, nz):
            line_sent(side, distance, 1)

    out = [[] for _ in range(parts)]
    for slot, p in enumerate(peers + [me]):
        rows = channel_ids(p)
        mid = jnp.dot(weight_ref[rows, :], pieces[...], preferred_element_type=jnp.float32)
        query = query_ref[rows, :].astype(jnp.float32)
        for l in range(local):
            lanes = slice(l * LANES, (l + 1) * LANES)
            mid_l, query_l, conv_l = mid[:, lanes], query[:, lanes], conv[l, rows, :]
            gate[l, rows, :] = query_l * mid_l
            grad_query[rows, lanes] = (mid_l * conv_l).astype(jnp.bfloat16)
            gated[rows, lanes] = (query_l * conv_l).astype(jnp.bfloat16)
        if slot < n - 1:
            out[0].append(push(gate.at[:, part_ids(p, 0), :], gate_full.at[0, slab_ids(me)], gate_sems, slot, {"seq": p}))
    for h in range(1, parts):
        out[h] = leave(gate, gate_full, gate_sems, h)
    own_slabs(gate, gate_full)

    def weight_half(which, dest):
        rows = pl.ds(pl.multiple_of(which * half, half), half)

        @pl.loop(0, n)
        def _(step):
            dest[step] = lax.dot_general(
                gated[rows, :], pieces[pl.ds(pl.multiple_of(step * cols, cols), cols), :],
                (((1,), (1,)), ((), ())), preferred_element_type=jnp.float32,
            )

    weight_half(1 - core, pair_send)
    pair = push(pair_send, pair_recv, pair_sems, 0, other)
    weight_half(core, own_part)

    home, ring = [], []
    for h in range(parts):
        for copy in out[h]:
            copy.wait()
        convolve(gate_full, h, True)
        home.extend(come_home(gate_full, turned, back_sems, h))
        if h == 0:
            pair.wait()
            for slot, p in enumerate(peers):
                ring_send[slot] = (own_part[p] + pair_recv[p]).astype(jnp.bfloat16)
                ring.append(push(ring_send.at[slot], ring_recv.at[slot], ring_sems, slot, {"seq": p}))

    total = own_part[me] + pair_recv[me]
    for slot, copy in enumerate(ring):
        copy.wait()
        total = total + ring_recv[slot].astype(jnp.float32)
    mine = pl.ds(pl.multiple_of(core * half, half), half)

    def chunk(p):
        return grad_weight.at[mine, pl.ds(pl.multiple_of(p * cols, cols), cols)]

    chunk(me)[...] = (total * scale).astype(jnp.bfloat16)
    share = [push(chunk(me), chunk(me), share_sems, slot, {"seq": p}) for slot, p in enumerate(peers)]
    final = [push(chunk(me), chunk(me), final_sems, n - 1, other)]

    for copy in home:
        copy.wait()
    for l in range(local):
        lanes = slice(l * LANES, (l + 1) * LANES)
        back = turned[l]
        grad_key[:, lanes] = (back * value_ref[:, lanes].astype(jnp.float32)).astype(jnp.bfloat16)
        grad_value[:, lanes] = (back * key_ref[:, lanes].astype(jnp.float32)).astype(jnp.bfloat16)
    for slot, copy in enumerate(share):
        copy.wait()
        source = lax.rem(me + n - slot - 1, n)
        final.append(push(chunk(source), chunk(source), final_sems, slot, other))
    for copy in final:
        copy.wait()


def sems(count):
    return pltpu.SemaphoreType.DMA((2, count))


def shards(query_proj, key_proj, value_proj, grad_out, out_weight, long_filter):
    n = lax.axis_size("seq")
    channels, positions = query_proj.shape[1:]
    local = positions // LANES
    slabs, width = local * n, channels // n
    nz = lax.axis_size("chan")
    parts = 2 if width % 32 == 0 else 1
    part_width = width // parts
    spec_rows = (slabs + 1) * part_width
    features = out_weight.shape[1]
    tables = [jnp.asarray(t) for t in make_tables(slabs)]
    f32, bf16 = jnp.float32, jnp.bfloat16
    scale = 1.0 / math.sqrt(lax.axis_size("dp") * long_filter.shape[1])
    half, cols = channels // 2, features // n
    vmem = pl.BlockSpec(memory_space=pltpu.VMEM)
    block = jax.ShapeDtypeStruct((channels, positions), bf16)
    rows = pltpu.VMEM((local, channels, LANES), f32)
    whole = pltpu.VMEM((parts, slabs, part_width, LANES), f32)
    grad_query, grad_key, grad_value, grad_weight = pl.pallas_call(
        functools.partial(kernel, n, nz, parts, scale),
        out_shape=(block, block, block, jax.ShapeDtypeStruct((channels, features), bf16)),
        in_specs=[vmem] * 12,
        out_specs=(vmem,) * 4,
        scratch_shapes=[
            pltpu.VMEM((features, positions), bf16),
            rows, whole, rows,
            pltpu.VMEM((parts, spec_rows, 2 * LANES), f32),
            pltpu.VMEM((spec_rows, 2 * LANES), f32),
            rows, whole, rows,
            pltpu.VMEM((channels, positions), bf16),
            pltpu.VMEM((n, half, cols), f32),
            pltpu.VMEM((n, half, cols), f32),
            pltpu.VMEM((n, half, cols), f32),
            pltpu.VMEM((n - 1, half, cols), bf16),
            pltpu.VMEM((n - 1, half, cols), bf16),
            sems(parts * (n - 1)), sems(parts * (n - 1)), sems(parts * (n - 1)), sems(parts * (n - 1)),
            sems(1), sems(n - 1), sems(n - 1), sems(n),
            pltpu.SemaphoreType.DMA((2, 2, nz - 1)),
            pltpu.SemaphoreType.DMA(()),
        ],
        compiler_params=pltpu.CompilerParams(
            collective_id=0, has_side_effects=True, vmem_limit_bytes=VMEM_LIMIT
        ),
        cost_estimate=pl.CostEstimate(
            flops=60 * parts * spec_rows * 256 * 256 + 4 * channels * features * positions,
            bytes_accessed=64 * channels * positions, transcendentals=0,
        ),
        name="hyena",
    )(query_proj[0], key_proj[0], value_proj[0], grad_out[0], out_weight, long_filter, *tables)
    return (grad_query[None], grad_key[None], grad_value[None], grad_weight.astype(f32))


def solution(mesh):
    placed = (
        P("dp", "chan", "seq"),
        P("dp", "chan", "seq"),
        P("dp", "chan", "seq"),
        P("dp", "chan", "seq"),
        P("chan", None),
        P(("chan", "seq"), None),
    )
    return jax.shard_map(
        shards,
        mesh=mesh,
        in_specs=placed,
        out_specs=(
            P("dp", "chan", "seq"),
            P("dp", "chan", "seq"),
            P("dp", "chan", "seq"),
            P("chan", None),
        ),
        check_vma=False,
    )
```
